512 devices in a mesh: dp: 64 (over z, y_lo, core), tensor: 8 (over y_hi, x).
Axes of the slice: x: 4, y: 4 (y_hi: 2, y_lo: 2; y = y_hi * 2 + y_lo), z: 16, core: 2. Of those that a mesh axis runs over, the one named last changes fastest.
Arguments:
- pooled: bfloat16 [16384, 1792], P(('dp', 'tensor')), as said below
- texts: bfloat16 [16384, 1792], P(('dp', 'tensor')), as said below
- head_w: bfloat16 [1792, 1792], P('tensor'), may hold values from -0.125 to 0.125
- log_scale: float32 [1], replicated, may hold values from 2.3 to 3.4
- bias: float32 [1], replicated, may hold values from -4 to -1
Outputs:
- grad_pooled: float32 [16384, 1792], P(('dp', 'tensor'))
- grad_head: float32 [1792, 1792], P('dp', 'tensor')
The draws below stay inside these ranges and needn't reach their ends.
Inputs may be any that keep to these rules, and one draw needn't show every extreme that they name: `pooled`: finite real values. `texts`: finite real values, no row zero.
All inputs are finite; a program needn't handle non-finite values.
Results may differ from the reference program's by a relative error of at most 0.025.
Values may be sent and summed in bfloat16 or wider, within the bound.
No kernel may reach another device: no remote copies, remote signals or barrier semaphores. Data moves between devices by JAX's collectives and lax.ppermute only.
A program may use at most 64 MiB of HBM per device.

```python
import math
import jax
import jax.numpy as jnp
from jax import lax

D = 1792
IMG_DEV = 256
IMAGES = 16384
TEXT_SUB = 32
N_DP = 64
N_TENSOR = 8


def draw_pooled(key, part):
    key = jax.random.fold_in(key, 5)
    key_rows, key_cols, key_base = jax.random.split(key, 3)
    row_scales = jnp.exp(jax.random.uniform(key_rows, (IMAGES, 1), jnp.float32, math.log(0.1), 0.0))
    col_scales = jnp.exp(jax.random.uniform(key_cols, (1, D), jnp.float32, math.log(0.1), 0.0))
    base = jnp.clip(jax.random.normal(key_base, (IMAGES, D), jnp.float32), -6.0, 6.0)
    return (2.0 * base * row_scales * col_scales).astype(jnp.bfloat16)


def draw_texts(key, part):
    key = jax.random.fold_in(key, 7)
    key_rows, key_cols, key_base = jax.random.split(key, 3)
    row_scales = jnp.exp(jax.random.uniform(key_rows, (IMAGES, 1), jnp.float32, 0.0, math.log(10.0)))
    col_scales = jnp.exp(jax.random.uniform(key_cols, (1, D), jnp.float32, 0.0, math.log(10.0)))
    base = jnp.clip(jax.random.normal(key_base, (IMAGES, D), jnp.float32), -6.0, 6.0)
    return (0.2 * base * row_scales * col_scales).astype(jnp.bfloat16)


def block_levels(own_key, extent, cuts, least, largest):
    level = 1.0
    for axis_at, blocks in cuts:
        draws = jax.random.uniform(jax.random.fold_in(jax.random.fold_in(own_key, 6), axis_at), (blocks,), jnp.float32, least / len(cuts), largest / len(cuts))
        level = level * jnp.repeat(jnp.exp(draws), extent[axis_at] // blocks).reshape((-1,) + (1,) * (len(extent) - 1 - axis_at))
    return level


def bell_draw(rng, dims, width, limit, cuts=(), held_as=jnp.bfloat16):
    gain = block_levels(rng, dims, cuts, -0.22, 0.18) if cuts else 1.0
    result = jax.random.normal(rng, dims, jnp.float32) * width * gain
    return jnp.minimum(jnp.maximum(result, -limit), limit).astype(held_as)


def setup_inputs(seed: int = 0) -> dict:
    key_list = jax.random.split(jax.random.key(seed), 6)
    return {
        "pooled": draw_pooled(jax.random.fold_in(key_list[5], 71), 0),
        "texts": draw_texts(jax.random.fold_in(key_list[5], 71), 0),
        "head_w": bell_draw(key_list[2], (D, D), D ** -0.5, 0.125, ((0, 8),)),
        "log_scale": jnp.clip(jax.random.uniform(key_list[3], (1,), jnp.float32, 2.3, 3.4), 2.3, 3.4),
        "bias": jnp.clip(jax.random.uniform(key_list[4], (1,), jnp.float32, -4.0, -1.0), -4.0, -1.0),
    }


def reference(pooled, texts, head_w, log_scale, bias):
    projected = lax.dot_general(pooled, head_w, (((1,), (1,)), ((), ())), preferred_element_type=jnp.float32).astype(jnp.bfloat16)
    proj_float = lax.optimization_barrier(projected).astype(jnp.float32)
    row_norms = jnp.sqrt(lax.optimization_barrier(jnp.sum(proj_float * proj_float, axis=1, keepdims=True)) + 1e-06)
    unit_rows = proj_float / row_norms
    embedded = unit_rows.astype(jnp.bfloat16)
    text_float = texts.astype(jnp.float32)
    text_unit = (text_float / jnp.sqrt(lax.optimization_barrier(jnp.sum(text_float * text_float, axis=1, keepdims=True)) + 1e-06)).astype(jnp.bfloat16)
    logit_scale = jnp.exp(log_scale[0])
    logit_bias = bias[0]
    grouped = text_unit.reshape(N_DP, N_TENSOR, TEXT_SUB, D).transpose(1, 0, 2, 3)
    grouped = grouped.reshape(N_TENSOR, N_DP * TEXT_SUB, D).astype(jnp.float32)
    group_ids = jnp.arange(IMAGES, dtype=jnp.int32).reshape(N_DP, N_TENSOR, TEXT_SUB).transpose(1, 0, 2)
    group_ids = group_ids.reshape(N_TENSOR, N_DP * TEXT_SUB)

    def one_shard(inputs):
        shard_embed, shard_index = inputs
        image_ids = shard_index * IMG_DEV + jnp.arange(IMG_DEV, dtype=jnp.int32)
        scores = jnp.einsum('id,tjd->itj', shard_embed.astype(jnp.float32), grouped)
        logits = logit_scale * scores + logit_bias
        labels = jnp.where(image_ids[:, None, None] == group_ids[None], 1.0, -1.0).astype(logits.dtype)
        pair_grad = (-labels * jax.nn.sigmoid(-labels * logits)).astype(jnp.bfloat16)
        pair_float = lax.optimization_barrier(pair_grad).astype(jnp.float32)
        partial_sum = jnp.einsum('itj,tjd->itd', pair_float, grouped)
        partial_sum = lax.optimization_barrier(partial_sum.astype(jnp.bfloat16)).astype(jnp.float32)
        return lax.optimization_barrier(jnp.sum(partial_sum, axis=1))
    text_terms = lax.map(one_shard, (embedded.reshape(N_DP, IMG_DEV, D), jnp.arange(N_DP, dtype=jnp.int32)))
    text_terms = text_terms.reshape(IMAGES, D)
    grad_embed = logit_scale * text_terms
    row_dots = lax.optimization_barrier(jnp.sum(unit_rows * grad_embed, axis=1, keepdims=True))
    grad_proj = ((grad_embed - unit_rows * row_dots) / row_norms).astype(jnp.bfloat16)
    col_count = D // N_TENSOR
    grad_pooled = jnp.zeros((IMAGES, D), jnp.float32)
    for column_block in range(N_TENSOR):
        first_col = column_block * col_count
        last_col = first_col + col_count
        block_term = jnp.dot(grad_proj[:, first_col:last_col], head_w[first_col:last_col, :], preferred_element_type=jnp.float32)
        grad_pooled = grad_pooled + lax.optimization_barrier(block_term.astype(jnp.bfloat16)).astype(jnp.float32)
    grad_head = jnp.dot(pooled.T, grad_proj, preferred_element_type=jnp.float32)
    return (grad_pooled, grad_head)
```

```python
import jax
import jax.numpy as jnp
from jax import lax
from jax.sharding import Mesh, PartitionSpec as P

BF = jnp.bfloat16
F32 = jnp.float32
T = ("yh", "x")
NZ, NYL, NC, NYH, NX = 16, 2, 2, 2, 4


def unit(v, axis):
    v = v.astype(F32)
    norms = jnp.sqrt(jnp.sum(v * v, axis=axis, keepdims=True) + 1e-06)
    return v / norms, norms


def gather_t(v):
    return lax.all_gather(lax.all_gather(v, "yh", axis=0, tiled=True), "x", axis=0, tiled=True)


def split_float(v):
    high = lax.reduce_precision(v, 8, 7)
    return high.astype(BF), (v - high).astype(BF)


def per_device(pooled, texts, head_w, log_scale, bias):
    z, yl, c = lax.axis_index("z"), lax.axis_index("yl"), lax.axis_index("c")
    yh, x = lax.axis_index("yh"), lax.axis_index("x")
    rows, width = pooled.shape
    cols = head_w.shape[0]
    scale = jnp.exp(log_scale[0])
    shift = bias[0]

    text_unit = unit(texts, 1)[0].astype(BF)
    text_pair = lax.all_gather(text_unit, "yl", axis=0, tiled=True)
    text_own = lax.all_gather(text_pair, "z", axis=0, tiled=True)
    text_other = lax.ppermute(text_own, "c", [(0, 1), (1, 0)])

    images = gather_t(pooled)
    count = images.shape[0]
    own_cols = lax.dot_general(
        head_w, images, (((1,), (1,)), ((), ())), preferred_element_type=F32
    ).astype(BF)
    proj = gather_t(own_cols).reshape(NX, NYH, cols, count)
    proj = proj.transpose(1, 0, 2, 3).reshape(width, count)
    unit_all, norms = unit(proj, 0)
    embedded = unit_all.astype(BF)

    small = width // (NZ * NYL * NC)
    padded = -(-small // 16) * 16
    parts = images.T.reshape(NZ, NYL * NC, small, count).transpose(1, 0, 2, 3)
    parts = jnp.pad(parts, ((0, 0), (0, 0), (0, padded - small), (0, 0)))
    parts = lax.all_to_all(parts, ("yl", "c"), split_axis=0, concat_axis=0, tiled=True)

    def half(text, masked):
        scores = jnp.dot(text, embedded, preferred_element_type=F32)
        logits = scale * scores + shift
        if masked:
            a = lax.broadcasted_iota(jnp.int32, logits.shape, 0) - (z * NYL + yl) * rows
            b = lax.broadcasted_iota(jnp.int32, logits.shape, 1) - (x * NYH + yh) * rows
            sign = jnp.where((a == b) & (a >= 0) & (a < rows), -1.0, 1.0).astype(F32)
            pair = (sign * jax.nn.sigmoid(sign * logits)).astype(BF)
        else:
            pair = jax.nn.sigmoid(logits).astype(BF)
        terms = lax.dot_general(
            text, pair, (((0,), (0,)), ((), ())), preferred_element_type=F32
        )
        return terms, jnp.sum(pair.astype(F32) * scores, axis=0)

    terms_own, dots_own = half(text_own, True)
    terms_other, dots_other = half(text_other, False)
    terms = (terms_own + terms_other).astype(BF).reshape(NYH * NX, cols, count)
    high, low = split_float(dots_own + dots_other)
    dots = jnp.stack([high, low] + [jnp.zeros_like(high)] * 14)
    block = jnp.concatenate([terms, jnp.broadcast_to(dots, (NYH * NX, 16, count))], axis=1)
    block = lax.all_to_all(block, T, split_axis=0, concat_axis=0, tiled=True)
    block = scale * jnp.sum(block.astype(F32), axis=0)
    row_dots = block[cols : cols + 1] + block[cols + 1 : cols + 2]
    own_unit = own_cols.astype(F32) / norms
    grad_proj = ((block[:cols] - own_unit * row_dots) / norms).astype(BF)

    grad_pooled = lax.dot_general(
        grad_proj, head_w, (((0,), (0,)), ((), ())), preferred_element_type=F32
    ).astype(BF)
    grad_pooled = lax.psum_scatter(grad_pooled, "x", scatter_dimension=0, tiled=True)
    grad_pooled = lax.psum_scatter(grad_pooled, "yh", scatter_dimension=0, tiled=True)

    grad_all = lax.all_gather(grad_proj, ("yl", "c"), axis=0)
    grad_head = jnp.einsum("szri,sfi->zrf", parts, grad_all, preferred_element_type=F32).astype(BF)
    grad_head = lax.all_to_all(grad_head, "z", split_axis=0, concat_axis=0, tiled=True)
    grad_head = jnp.sum(grad_head.astype(F32), axis=0)[:small]
    return (grad_pooled.astype(F32), grad_head)


def solution(mesh):
    fine = Mesh(mesh.devices.reshape(NZ, NYL, NC, NYH, NX), ("z", "yl", "c", "yh", "x"))
    dp = ("z", "yl", "c")
    rows = P(dp + T, None)
    return jax.shard_map(
        per_device,
        mesh=fine,
        in_specs=(rows, rows, P(T, None), P(), P()),
        out_specs=(rows, P(dp, T)),
        check_vma=False,
    )
```

```python
import jax
import jax.numpy as jnp
from jax import lax
from jax.sharding import Mesh, PartitionSpec as P

BF = jnp.bfloat16
F32 = jnp.float32
T = ("yh", "x")
NZ, NYL, NC, NYH, NX = 16, 2, 2, 2, 4


def unit(v, axis):
    v = v.astype(F32)
    norms = jnp.sqrt(jnp.sum(v * v, axis=axis, keepdims=True) + 1e-06)
    return v / norms, norms


def gather_t(v):
    return lax.all_gather(lax.all_gather(v, "yh", axis=0, tiled=True), "x", axis=0, tiled=True)


def split_float(v):
    high = lax.reduce_precision(v, 8, 7)
    return high.astype(BF), (v - high).astype(BF)


def per_device(pooled, texts, head_w, log_scale, bias):
    z, yl, c = lax.axis_index("z"), lax.axis_index("yl"), lax.axis_index("c")
    yh, x = lax.axis_index("yh"), lax.axis_index("x")
    rows, width = pooled.shape
    cols = head_w.shape[0]
    scale = jnp.exp(log_scale[0])
    shift = bias[0]

    text_unit = unit(texts, 1)[0].astype(BF)
    text_pair = lax.all_gather(text_unit, "yl", axis=0, tiled=True)
    text_own = lax.all_gather(text_pair, "z", axis=0, tiled=True)

    images = gather_t(pooled)
    count = images.shape[0]
    own_cols = lax.dot_general(
        head_w, images, (((1,), (1,)), ((), ())), preferred_element_type=F32
    ).astype(BF)
    proj = gather_t(own_cols).reshape(NX, NYH, cols, count)
    proj = proj.transpose(1, 0, 2, 3).reshape(width, count)
    unit_all, norms = unit(proj, 0)
    embedded = unit_all.astype(BF)

    small = width // (NZ * NYL * NC)
    padded = -(-small // 16) * 16
    parts = images.T.reshape(NZ, NYL * NC, small, count).transpose(1, 0, 2, 3)
    parts = jnp.pad(parts, ((0, 0), (0, 0), (0, padded - small), (0, 0)))
    parts = lax.all_to_all(parts, ("yl", "c"), split_axis=0, concat_axis=0, tiled=True)

    text_own, embedded, norms, parts = lax.optimization_barrier(
        (text_own, embedded, norms, parts)
    )
    text_other = lax.ppermute(text_own, "c", [(0, 1), (1, 0)])

    def half(text, masked):
        scores = jnp.dot(text, embedded, preferred_element_type=F32)
        logits = scale * scores + shift
        if masked:
            a = lax.broadcasted_iota(jnp.int32, logits.shape, 0) - (z * NYL + yl) * rows
            b = lax.broadcasted_iota(jnp.int32, logits.shape, 1) - (x * NYH + yh) * rows
            sign = jnp.where((a == b) & (a >= 0) & (a < rows), -1.0, 1.0).astype(F32)
            pair = (sign * jax.nn.sigmoid(sign * logits)).astype(BF)
        else:
            pair = jax.nn.sigmoid(logits).astype(BF)
        terms = lax.dot_general(
            text, pair, (((0,), (0,)), ((), ())), preferred_element_type=F32
        )
        return terms, jnp.sum(pair.astype(F32) * scores, axis=0)

    terms_own, dots_own = half(text_own, True)
    terms_other, dots_other = half(text_other, False)
    terms = (terms_own + terms_other).astype(BF).reshape(NYH * NX, cols, count)
    high, low = split_float(dots_own + dots_other)
    dots = jnp.stack([high, low] + [jnp.zeros_like(high)] * 14)
    block = jnp.concatenate([terms, jnp.broadcast_to(dots, (NYH * NX, 16, count))], axis=1)
    block = lax.all_to_all(block, T, split_axis=0, concat_axis=0, tiled=True)
    block = scale * jnp.sum(block.astype(F32), axis=0)
    row_dots = block[cols : cols + 1] + block[cols + 1 : cols + 2]
    own_unit = own_cols.astype(F32) / norms
    grad_proj = ((block[:cols] - own_unit * row_dots) / norms).astype(BF)

    grad_pooled = lax.dot_general(
        grad_proj, head_w, (((0,), (0,)), ((), ())), preferred_element_type=F32
    ).astype(BF)
    grad_pooled = lax.psum_scatter(grad_pooled, "x", scatter_dimension=0, tiled=True)
    grad_pooled = lax.psum_scatter(grad_pooled, "yh", scatter_dimension=0, tiled=True)

    grad_all = lax.all_gather(grad_proj, ("yl", "c"), axis=0)
    grad_head = jnp.einsum("szri,sfi->zrf", parts, grad_all, preferred_element_type=F32).astype(BF)
    grad_head = lax.all_to_all(grad_head, "z", split_axis=0, concat_axis=0, tiled=True)
    grad_head = jnp.sum(grad_head.astype(F32), axis=0)[:small]
    return (grad_pooled.astype(F32), grad_head)


def solution(mesh):
    fine = Mesh(mesh.devices.reshape(NZ, NYL, NC, NYH, NX), ("z", "yl", "c", "yh", "x"))
    dp = ("z", "yl", "c")
    rows = P(dp + T, None)
    return jax.shard_map(
        per_device,
        mesh=fine,
        in_specs=(rows, rows, P(T, None), P(), P()),
        out_specs=(rows, P(dp, T)),
        check_vma=False,
    )
```

```python
import jax
import jax.numpy as jnp
from jax import lax
from jax.experimental import pallas as pl
from jax.experimental.pallas import tpu as pltpu
from jax.sharding import Mesh, PartitionSpec as P

BF = jnp.bfloat16
F32 = jnp.float32
T = ("yh", "x")
NZ, NYL, NC, NYH, NX = 16, 2, 2, 2, 4
CORES = [(0, 1), (1, 0)]


def unit(v, axis):
    v = v.astype(F32)
    norms = jnp.sqrt(jnp.sum(v * v, axis=axis, keepdims=True) + 1e-06)
    return v / norms, norms


def gather_t(v):
    return lax.all_gather(lax.all_gather(v, "yh", axis=0, tiled=True), "x", axis=0, tiled=True)


def unit_kernel(rows_ref, out_ref):
    v = rows_ref[...].astype(F32)
    out_ref[...] = (v / jnp.sqrt(jnp.sum(v * v, axis=1, keepdims=True) + 1e-06)).astype(BF)


def pairs_kernel(own, rows, par_ref, pos_ref, text_ref, image_ref, out_ref):
    text = text_ref[...]
    scores = lax.dot_general(
        image_ref[...], text, (((1,), (1,)), ((), ())), preferred_element_type=F32
    )
    logits = par_ref[0] * scores + par_ref[1]
    if own:
        a = lax.broadcasted_iota(jnp.int32, scores.shape, 1) - pos_ref[0]
        b = lax.broadcasted_iota(jnp.int32, scores.shape, 0) - pos_ref[1]
        sign = jnp.where((a == b) & (a >= 0) & (a < rows), -1.0, 1.0)
        pair = sign / (1.0 + jnp.exp(-sign * logits))
    else:
        pair = 1.0 / (1.0 + jnp.exp(-logits))
    pair = pair.astype(BF)
    dots = jnp.sum(pair.astype(F32) * scores, axis=1, keepdims=True)
    terms = jnp.dot(pair, text, preferred_element_type=F32)
    width = terms.shape[1]
    lane = lax.broadcasted_iota(jnp.int32, (terms.shape[0], 128), 1)
    if own:
        tail = jnp.where(lane == 0, dots, 0.0)
    else:
        high = dots.astype(BF).astype(F32)
        tail = jnp.where(lane == 0, high, jnp.where(lane == 1, dots - high, 0.0))
    out_ref[:width] = terms.T.astype(out_ref.dtype)
    out_ref[width:] = tail.T[:16].astype(out_ref.dtype)


def pairs(own, rows, par, pos, text, image):
    count, width = image.shape
    smem = pl.BlockSpec(memory_space=pltpu.SMEM)
    vmem = pl.BlockSpec(memory_space=pltpu.VMEM)
    return pl.pallas_call(
        lambda *refs: pairs_kernel(own, rows, *refs),
        in_specs=[smem, smem, vmem, vmem],
        out_specs=vmem,
        out_shape=jax.ShapeDtypeStruct((width + 16, count), F32 if own else BF),
        compiler_params=pltpu.CompilerParams(vmem_limit_bytes=40 * 2**20),
        cost_estimate=pl.CostEstimate(
            flops=4 * count * width * text.shape[0],
            bytes_accessed=2 * width * (text.shape[0] + 2 * count),
            transcendentals=count * text.shape[0],
        ),
        name="pairs_own" if own else "pairs_other",
    )(par, pos, text, image)


def join_kernel(own_ref, other_ref, out_ref):
    blocks, height, _ = out_ref.shape
    cols = height - 16
    total = own_ref[blocks * cols :] + other_ref[blocks * cols :].astype(F32)
    dots = total[0:1] + total[1:2]
    high = dots.astype(BF).astype(F32)
    row = lax.broadcasted_iota(jnp.int32, total.shape, 0)
    tail = jnp.where(row == 0, high, jnp.where(row == 1, dots - high, 0.0)).astype(BF)
    for t in range(blocks):
        part = pl.ds(t * cols, cols)
        out_ref[t, :cols] = (own_ref[part] + other_ref[part].astype(F32)).astype(BF)
        out_ref[t, cols:] = tail


def per_device(pooled, texts, head_w, log_scale, bias):
    z, yl, c = lax.axis_index("z"), lax.axis_index("yl"), lax.axis_index("c")
    yh, x = lax.axis_index("yh"), lax.axis_index("x")
    rows, width = pooled.shape
    cols = head_w.shape[0]
    scale = jnp.exp(log_scale[0])
    shift = bias[0]

    text_unit = pl.pallas_call(
        unit_kernel, out_shape=jax.ShapeDtypeStruct(texts.shape, BF), name="unit_texts"
    )(texts)
    text_pair = lax.all_gather(text_unit, "yl", axis=0, tiled=True)
    text_own = lax.all_gather(text_pair, "z", axis=0, tiled=True)

    images = gather_t(pooled)
    count = images.shape[0]
    own_cols = lax.dot_general(
        head_w, images, (((1,), (1,)), ((), ())), preferred_element_type=F32
    ).astype(BF)
    proj = gather_t(own_cols).reshape(NX, NYH, cols, count)
    proj = proj.transpose(1, 0, 2, 3).reshape(width, count)
    unit_all, norms = unit(proj, 0)
    embedded = unit_all.astype(BF).T
    embedded_other = lax.ppermute(embedded, "c", CORES)

    small = width // (NZ * NYL * NC)
    padded = -(-small // 16) * 16
    parts = images.T.reshape(NZ, NYL * NC, small, count).transpose(1, 0, 2, 3)
    parts = jnp.pad(parts, ((0, 0), (0, 0), (0, padded - small), (0, 0)))
    parts = lax.all_to_all(parts, ("yl", "c"), split_axis=0, concat_axis=0, tiled=True)

    text_own, embedded, embedded_other, norms, parts = lax.optimization_barrier(
        (text_own, embedded, embedded_other, norms, parts)
    )
    par = jnp.stack([scale, shift])
    pos = jnp.stack([(z * NYL + yl) * rows, (x * NYH + yh) * rows]).astype(jnp.int32)
    terms_other = pairs(False, rows, par, pos, text_own, embedded_other)
    terms_other = lax.ppermute(terms_other, "c", CORES)
    terms_own = pairs(True, rows, par, pos, text_own, embedded)
    block = pl.pallas_call(
        join_kernel,
        out_shape=jax.ShapeDtypeStruct((NYH * NX, cols + 16, count), BF),
        compiler_params=pltpu.CompilerParams(vmem_limit_bytes=40 * 2**20),
        name="join_cores",
    )(terms_own, terms_other)
    block = lax.all_to_all(block, T, split_axis=0, concat_axis=0, tiled=True)
    block = scale * jnp.sum(block.astype(F32), axis=0)
    row_dots = block[cols : cols + 1] + block[cols + 1 : cols + 2]
    own_unit = own_cols.astype(F32) / norms
    grad_proj = ((block[:cols] - own_unit * row_dots) / norms).astype(BF)

    grad_pooled = lax.dot_general(
        grad_proj, head_w, (((0,), (0,)), ((), ())), preferred_element_type=F32
    ).astype(BF)
    grad_pooled = grad_pooled.reshape(NX * NYH, rows, width)
    grad_pooled = lax.all_to_all(grad_pooled, ("x", "yh"), split_axis=0, concat_axis=0, tiled=True)
    grad_pooled = jnp.sum(grad_pooled.astype(F32), axis=0)

    grad_all = lax.all_gather(grad_proj, ("yl", "c"), axis=0)
    grad_head = jnp.einsum("szri,sfi->zrf", parts, grad_all, preferred_element_type=F32).astype(BF)
    grad_head = lax.all_to_all(grad_head, "z", split_axis=0, concat_axis=0, tiled=True)
    grad_head = jnp.sum(grad_head.astype(F32), axis=0)[:small]
    return (grad_pooled, grad_head)


def solution(mesh):
    fine = Mesh(mesh.devices.reshape(NZ, NYL, NC, NYH, NX), ("z", "yl", "c", "yh", "x"))
    dp = ("z", "yl", "c")
    rows = P(dp + T, None)
    return jax.shard_map(
        per_device,
        mesh=fine,
        in_specs=(rows, rows, P(T, None), P(), P()),
        out_specs=(rows, P(dp, T)),
        check_vma=False,
    )
```

```python
import jax
import jax.numpy as jnp
from jax import lax
from jax.experimental import pallas as pl
from jax.experimental.pallas import tpu as pltpu
from jax.sharding import Mesh, PartitionSpec as P

BF = jnp.bfloat16
F32 = jnp.float32
T = ("yh", "x")
NZ, NYL, NC, NYH, NX = 16, 2, 2, 2, 4
CORES = [(0, 1), (1, 0)]


def unit(v, axis):
    v = v.astype(F32)
    norms = jnp.sqrt(jnp.sum(v * v, axis=axis, keepdims=True) + 1e-06)
    return v / norms, norms


def gather_t(v):
    return lax.all_gather(lax.all_gather(v, "yh", axis=0, tiled=True), "x", axis=0, tiled=True)


def unit_kernel(rows_ref, out_ref):
    v = rows_ref[...].astype(F32)
    out_ref[...] = (v / jnp.sqrt(jnp.sum(v * v, axis=1, keepdims=True) + 1e-06)).astype(BF)


def pairs_kernel(own, rows, par_ref, pos_ref, text_ref, image_ref, out_ref):
    text = text_ref[...]
    scores = lax.dot_general(
        image_ref[...], text, (((1,), (1,)), ((), ())), preferred_element_type=F32
    )
    logits = par_ref[0] * scores + par_ref[1]
    if own:
        a = lax.broadcasted_iota(jnp.int32, scores.shape, 1) - pos_ref[0]
        b = lax.broadcasted_iota(jnp.int32, scores.shape, 0) - pos_ref[1]
        sign = jnp.where((a == b) & (a >= 0) & (a < rows), -1.0, 1.0)
        pair = sign / (1.0 + jnp.exp(-sign * logits))
    else:
        pair = 1.0 / (1.0 + jnp.exp(-logits))
    pair = pair.astype(BF)
    dots = jnp.sum(pair.astype(F32) * scores, axis=1, keepdims=True)
    terms = jnp.dot(pair, text, preferred_element_type=F32)
    width = terms.shape[1]
    lane = lax.broadcasted_iota(jnp.int32, (terms.shape[0], 128), 1)
    if own:
        tail = jnp.where(lane == 0, dots, 0.0)
    else:
        high = dots.astype(BF).astype(F32)
        tail = jnp.where(lane == 0, high, jnp.where(lane == 1, dots - high, 0.0))
    out_ref[:width] = terms.T.astype(out_ref.dtype)
    out_ref[width:] = tail.T[:16].astype(out_ref.dtype)


def pairs(own, rows, par, pos, text, image):
    count, width = image.shape
    smem = pl.BlockSpec(memory_space=pltpu.SMEM)
    vmem = pl.BlockSpec(memory_space=pltpu.VMEM)
    return pl.pallas_call(
        lambda *refs: pairs_kernel(own, rows, *refs),
        in_specs=[smem, smem, vmem, vmem],
        out_specs=vmem,
        out_shape=jax.ShapeDtypeStruct((width + 16, count), F32 if own else BF),
        compiler_params=pltpu.CompilerParams(vmem_limit_bytes=40 * 2**20),
        cost_estimate=pl.CostEstimate(
            flops=4 * count * width * text.shape[0],
            bytes_accessed=2 * width * (text.shape[0] + 2 * count),
            transcendentals=count * text.shape[0],
        ),
        name="pairs_own" if own else "pairs_other",
    )(par, pos, text, image)


def join_kernel(own_ref, other_ref, out_ref):
    blocks, height, _ = out_ref.shape
    cols = height - 16
    total = own_ref[blocks * cols :] + other_ref[blocks * cols :].astype(F32)
    dots = total[0:1] + total[1:2]
    high = dots.astype(BF).astype(F32)
    row = lax.broadcasted_iota(jnp.int32, total.shape, 0)
    tail = jnp.where(row == 0, high, jnp.where(row == 1, dots - high, 0.0)).astype(BF)
    for t in range(blocks):
        part = pl.ds(t * cols, cols)
        out_ref[t, :cols] = (own_ref[part] + other_ref[part].astype(F32)).astype(BF)
        out_ref[t, cols:] = tail


def per_device(pooled, texts, head_w, log_scale, bias):
    z, yl, c = lax.axis_index("z"), lax.axis_index("yl"), lax.axis_index("c")
    yh, x = lax.axis_index("yh"), lax.axis_index("x")
    rows, width = pooled.shape
    cols = head_w.shape[0]
    scale = jnp.exp(log_scale[0])
    shift = bias[0]

    text_unit = pl.pallas_call(
        unit_kernel, out_shape=jax.ShapeDtypeStruct(texts.shape, BF), name="unit_texts"
    )(texts)
    text_pair = lax.all_gather(text_unit, "yl", axis=0, tiled=True)
    text_own = lax.all_gather(text_pair, "z", axis=0, tiled=True)

    images = gather_t(pooled)
    count = images.shape[0]
    own_cols = lax.dot_general(
        head_w, images, (((1,), (1,)), ((), ())), preferred_element_type=F32
    ).astype(BF)
    proj = gather_t(own_cols).reshape(NX, NYH, cols, count)
    proj = proj.transpose(1, 0, 2, 3).reshape(width, count)
    unit_all, norms = unit(proj, 0)
    embedded = unit_all.astype(BF).T
    embedded_other = lax.ppermute(embedded, "c", CORES)

    small = width // (NZ * NYL * NC)
    padded = -(-small // 16) * 16
    parts = images.T.reshape(NZ, NYL * NC, small, count).transpose(1, 0, 2, 3)
    parts = jnp.pad(parts, ((0, 0), (0, 0), (0, padded - small), (0, 0)))
    parts = lax.all_to_all(parts, ("yl", "c"), split_axis=0, concat_axis=0, tiled=True)

    text_own, embedded, embedded_other, norms, parts = lax.optimization_barrier(
        (text_own, embedded, embedded_other, norms, parts)
    )
    par = jnp.stack([scale, shift])
    pos = jnp.stack([(z * NYL + yl) * rows, (x * NYH + yh) * rows]).astype(jnp.int32)
    terms_other = pairs(False, rows, par, pos, text_own, embedded_other)
    terms_other = lax.ppermute(terms_other, "c", CORES)
    terms_own = pairs(True, rows, par, pos, text_own, embedded)
    block = pl.pallas_call(
        join_kernel,
        out_shape=jax.ShapeDtypeStruct((NYH * NX, cols + 16, count), BF),
        compiler_params=pltpu.CompilerParams(vmem_limit_bytes=40 * 2**20),
        name="join_cores",
    )(terms_own, terms_other)
    block = lax.all_to_all(block, T, split_axis=0, concat_axis=0, tiled=True)
    block = scale * jnp.sum(block.astype(F32), axis=0)
    row_dots = block[cols : cols + 1] + block[cols + 1 : cols + 2]
    own_unit = own_cols.astype(F32) / norms
    grad_proj = ((block[:cols] - own_unit * row_dots) / norms).astype(BF)

    grad_pooled = lax.dot_general(
        grad_proj, head_w, (((0,), (0,)), ((), ())), preferred_element_type=F32
    ).astype(BF)
    grad_pooled = lax.psum_scatter(grad_pooled, "x", scatter_dimension=0, tiled=True)
    given = jnp.where(yh == 0, grad_pooled[rows:], grad_pooled[:rows])
    taken = lax.ppermute(given, "yh", CORES)
    kept = jnp.where(yh == 0, grad_pooled[:rows], grad_pooled[rows:])
    grad_pooled = kept.astype(F32) + taken.astype(F32)

    grad_all = lax.all_gather(grad_proj, ("yl", "c"), axis=0)
    grad_head = jnp.einsum("szri,sfi->zrf", parts, grad_all, preferred_element_type=F32).astype(BF)
    grad_head = lax.all_to_all(grad_head, "z", split_axis=0, concat_axis=0, tiled=True)
    grad_head = jnp.sum(grad_head.astype(F32), axis=0)[:small]
    return (grad_pooled, grad_head)


def solution(mesh):
    fine = Mesh(mesh.devices.reshape(NZ, NYL, NC, NYH, NX), ("z", "yl", "c", "yh", "x"))
    dp = ("z", "yl", "c")
    rows = P(dp + T, None)
    return jax.shard_map(
        per_device,
        mesh=fine,
        in_specs=(rows, rows, P(T, None), P(), P()),
        out_specs=(rows, P(dp, T)),
        check_vma=False,
    )
```

```python
import jax
import jax.numpy as jnp
from jax import lax
from jax.experimental import pallas as pl
from jax.experimental.pallas import tpu as pltpu
from jax.sharding import Mesh, PartitionSpec as P

BF = jnp.bfloat16
F32 = jnp.float32
T = ("yh", "x")
NZ, NYL, NC, NYH, NX = 16, 2, 2, 2, 4
CORES = [(0, 1), (1, 0)]


def unit(v, axis):
    v = v.astype(F32)
    norms = jnp.sqrt(jnp.sum(v * v, axis=axis, keepdims=True) + 1e-06)
    return v / norms, norms


def gather_t(v):
    return lax.all_gather(lax.all_gather(v, "yh", axis=0, tiled=True), "x", axis=0, tiled=True)


def unit_kernel(rows_ref, out_ref):
    v = rows_ref[...].astype(F32)
    out_ref[...] = (v / jnp.sqrt(jnp.sum(v * v, axis=1, keepdims=True) + 1e-06)).astype(BF)


def pairs_kernel(own, rows, par_ref, pos_ref, text_ref, image_ref, out_ref):
    text = text_ref[...]
    scores = lax.dot_general(
        image_ref[...], text, (((1,), (1,)), ((), ())), preferred_element_type=F32
    )
    logits = par_ref[0] * scores + par_ref[1]
    if own:
        a = lax.broadcasted_iota(jnp.int32, scores.shape, 1) - pos_ref[0]
        b = lax.broadcasted_iota(jnp.int32, scores.shape, 0) - pos_ref[1]
        sign = jnp.where((a == b) & (a >= 0) & (a < rows), -1.0, 1.0)
        pair = sign / (1.0 + jnp.exp(-sign * logits))
    else:
        pair = 1.0 / (1.0 + jnp.exp(-logits))
    pair = pair.astype(BF)
    dots = jnp.sum(pair.astype(F32) * scores, axis=1, keepdims=True)
    terms = jnp.dot(pair, text, preferred_element_type=F32)
    width = terms.shape[1]
    lane = lax.broadcasted_iota(jnp.int32, (terms.shape[0], 128), 1)
    if own:
        tail = jnp.where(lane == 0, dots, 0.0)
    else:
        high = dots.astype(BF).astype(F32)
        tail = jnp.where(lane == 0, high, jnp.where(lane == 1, dots - high, 0.0))
    out_ref[:width] = terms.T.astype(out_ref.dtype)
    out_ref[width:] = tail.T[:16].astype(out_ref.dtype)


def pairs(own, rows, par, pos, text, image):
    count, width = image.shape
    smem = pl.BlockSpec(memory_space=pltpu.SMEM)
    vmem = pl.BlockSpec(memory_space=pltpu.VMEM)
    return pl.pallas_call(
        lambda *refs: pairs_kernel(own, rows, *refs),
        in_specs=[smem, smem, vmem, vmem],
        out_specs=vmem,
        out_shape=jax.ShapeDtypeStruct((width + 16, count), F32 if own else BF),
        compiler_params=pltpu.CompilerParams(vmem_limit_bytes=40 * 2**20),
        cost_estimate=pl.CostEstimate(
            flops=4 * count * width * text.shape[0],
            bytes_accessed=2 * width * (text.shape[0] + 2 * count),
            transcendentals=count * text.shape[0],
        ),
        name="pairs_own" if own else "pairs_other",
    )(par, pos, text, image)


def score(image, text):
    return lax.dot_general(image, text, (((1,), (1,)), ((), ())), preferred_element_type=F32)


def head_kernel(parts_ref, grads_ref, out_ref):
    sources, blocks, height, count = parts_ref.shape
    cols = out_ref.shape[2]
    total = jnp.zeros((blocks * height, cols), F32)
    for s in range(sources):
        total += score(parts_ref[s].reshape(blocks * height, count), grads_ref[pl.ds(s * cols, cols)])
    out_ref[...] = total.astype(BF).reshape(out_ref.shape)


def join_kernel(own_ref, other_ref, out_ref):
    blocks, height, _ = out_ref.shape
    cols = height - 16
    total = own_ref[blocks * cols :] + other_ref[blocks * cols :].astype(F32)
    dots = total[0:1] + total[1:2]
    high = dots.astype(BF).astype(F32)
    row = lax.broadcasted_iota(jnp.int32, total.shape, 0)
    tail = jnp.where(row == 0, high, jnp.where(row == 1, dots - high, 0.0)).astype(BF)
    for t in range(blocks):
        part = pl.ds(t * cols, cols)
        out_ref[t, :cols] = (own_ref[part] + other_ref[part].astype(F32)).astype(BF)
        out_ref[t, cols:] = tail


def per_device(pooled, texts, head_w, log_scale, bias):
    z, yl, c = lax.axis_index("z"), lax.axis_index("yl"), lax.axis_index("c")
    yh, x = lax.axis_index("yh"), lax.axis_index("x")
    rows, width = pooled.shape
    cols = head_w.shape[0]
    scale = jnp.exp(log_scale[0])
    shift = bias[0]

    text_unit = pl.pallas_call(
        unit_kernel, out_shape=jax.ShapeDtypeStruct(texts.shape, BF), name="unit_texts"
    )(texts)
    text_pair = lax.all_gather(text_unit, "yl", axis=0, tiled=True)
    text_own = lax.all_gather(text_pair, "z", axis=0, tiled=True)

    images = gather_t(pooled)
    count = images.shape[0]
    own_cols = lax.dot_general(
        head_w, images, (((1,), (1,)), ((), ())), preferred_element_type=F32
    ).astype(BF)
    proj = gather_t(own_cols).reshape(NX, NYH, cols, count)
    proj = proj.transpose(1, 0, 2, 3).reshape(width, count)
    unit_all, norms = unit(proj, 0)
    embedded = unit_all.astype(BF).T
    embedded_other = lax.ppermute(embedded, "c", CORES)

    small = width // (NZ * NYL * NC)
    padded = -(-small // 16) * 16
    parts = images.T.reshape(NZ, NYL * NC, small, count).transpose(1, 0, 2, 3)
    parts = jnp.pad(parts, ((0, 0), (0, 0), (0, padded - small), (0, 0)))
    parts = lax.all_to_all(parts, ("yl", "c"), split_axis=0, concat_axis=0, tiled=True)

    text_own, embedded, embedded_other, norms, parts = lax.optimization_barrier(
        (text_own, embedded, embedded_other, norms, parts)
    )
    par = jnp.stack([scale, shift])
    pos = jnp.stack([(z * NYL + yl) * rows, (x * NYH + yh) * rows]).astype(jnp.int32)
    terms_other = pairs(False, rows, par, pos, text_own, embedded_other)
    terms_other = lax.ppermute(terms_other, "c", CORES)
    terms_own = pairs(True, rows, par, pos, text_own, embedded)
    block = pl.pallas_call(
        join_kernel,
        out_shape=jax.ShapeDtypeStruct((NYH * NX, cols + 16, count), BF),
        compiler_params=pltpu.CompilerParams(vmem_limit_bytes=40 * 2**20),
        name="join_cores",
    )(terms_own, terms_other)
    block = lax.all_to_all(block, T, split_axis=0, concat_axis=0, tiled=True)
    block = scale * jnp.sum(block.astype(F32), axis=0)
    row_dots = block[cols : cols + 1] + block[cols + 1 : cols + 2]
    own_unit = own_cols.astype(F32) / norms
    grad_proj = ((block[:cols] - own_unit * row_dots) / norms).astype(BF)

    grad_pooled = lax.dot_general(
        grad_proj, head_w, (((0,), (0,)), ((), ())), preferred_element_type=F32
    ).astype(BF)
    grad_pooled = lax.psum_scatter(grad_pooled, "x", scatter_dimension=0, tiled=True)
    given = jnp.where(yh == 0, grad_pooled[rows:], grad_pooled[:rows])
    kept = jnp.where(yh == 0, grad_pooled[:rows], grad_pooled[rows:])
    given, kept = lax.optimization_barrier((given, kept))
    taken = lax.ppermute(given, "yh", CORES)
    grad_pooled = kept.astype(F32) + taken.astype(F32)

    grad_all = lax.all_gather(grad_proj, ("yl", "c"), axis=0, tiled=True)
    grad_head = pl.pallas_call(
        head_kernel,
        out_shape=jax.ShapeDtypeStruct((NZ, padded, cols), BF),
        compiler_params=pltpu.CompilerParams(vmem_limit_bytes=40 * 2**20),
        cost_estimate=pl.CostEstimate(
            flops=2 * NZ * padded * cols * count * NYL * NC,
            bytes_accessed=2 * (parts.size + grad_all.size + NZ * padded * cols),
            transcendentals=0,
        ),
        name="head_product",
    )(parts, grad_all)
    grad_head = lax.all_to_all(grad_head, "z", split_axis=0, concat_axis=0, tiled=True)
    grad_head, grad_pooled = lax.optimization_barrier((grad_head, grad_pooled))
    grad_head = jnp.sum(grad_head.astype(F32), axis=0)[:small]
    return (grad_pooled, grad_head)


def solution(mesh):
    fine = Mesh(mesh.devices.reshape(NZ, NYL, NC, NYH, NX), ("z", "yl", "c", "yh", "x"))
    dp = ("z", "yl", "c")
    rows = P(dp + T, None)
    return jax.shard_map(
        per_device,
        mesh=fine,
        in_specs=(rows, rows, P(T, None), P(), P()),
        out_specs=(rows, P(dp, T)),
        check_vma=False,
    )
```

```python
import jax
import jax.numpy as jnp
from jax import lax
from jax.experimental import pallas as pl
from jax.experimental.pallas import tpu as pltpu
from jax.sharding import Mesh, PartitionSpec as P

BF = jnp.bfloat16
F32 = jnp.float32
T = ("yh", "x")
NZ, NYL, NC, NYH, NX = 16, 2, 2, 2, 4
CORES = [(0, 1), (1, 0)]


def unit(v, axis):
    v = v.astype(F32)
    norms = jnp.sqrt(jnp.sum(v * v, axis=axis, keepdims=True) + 1e-06)
    return v / norms, norms


def gather_t(v):
    return lax.all_gather(lax.all_gather(v, "yh", axis=0, tiled=True), "x", axis=0, tiled=True)


def unit_kernel(rows_ref, out_ref):
    v = rows_ref[...].astype(F32)
    out_ref[...] = (v / jnp.sqrt(jnp.sum(v * v, axis=1, keepdims=True) + 1e-06)).astype(BF)


def score(image, text):
    return lax.dot_general(image, text, (((1,), (1,)), ((), ())), preferred_element_type=F32)


def head_kernel(parts_ref, grads_ref, out_ref):
    sources, blocks, height, count = parts_ref.shape
    cols = grads_ref.shape[0] // sources
    total = jnp.zeros((blocks * height, cols), F32)
    for s in range(sources):
        total += score(parts_ref[s].reshape(blocks * height, count), grads_ref[pl.ds(s * cols, cols)])
    total = total.reshape(blocks, height, cols)[:, : out_ref.shape[1] // 2]
    rest = jnp.concatenate(
        [total[:, :, 128:], jnp.zeros((*total.shape[:2], 256 - cols), F32)], axis=2
    )
    out_ref[...] = jnp.concatenate([total[:, :, :128], rest], axis=1).astype(BF)


def pairs_kernel(rows, par_ref, pos_ref, text_hbm, image_hbm, out_ref, text_ref, image_ref, sems):
    chunks = sems.shape[0] - 1
    step = text_ref.shape[0] // chunks
    copies = [
        pltpu.make_async_copy(
            text_hbm.at[pl.ds(k * step, step)], text_ref.at[pl.ds(k * step, step)], sems.at[k]
        )
        for k in range(chunks)
    ]
    image_copy = pltpu.make_async_copy(image_hbm, image_ref, sems.at[chunks])
    image_copy.start()
    for copy in copies:
        copy.start()
    image_copy.wait()
    image = image_ref[...]
    terms = dots = None
    for k, copy in enumerate(copies):
        copy.wait()
        text = text_ref[pl.ds(k * step, step)]
        scores = score(image, text)
        logits = par_ref[0] * scores + par_ref[1]
        a = lax.broadcasted_iota(jnp.int32, scores.shape, 1) + (k * step - pos_ref[0])
        b = lax.broadcasted_iota(jnp.int32, scores.shape, 0) - pos_ref[1]
        sign = jnp.where((a == b) & (a >= 0) & (a < rows), -1.0, 1.0)
        pair = (sign / (1.0 + jnp.exp(-sign * logits))).astype(BF)
        dot = jnp.sum(pair.astype(F32) * scores, axis=1, keepdims=True)
        term = jnp.dot(pair, text, preferred_element_type=F32)
        terms = term if k == 0 else terms + term
        dots = dot if k == 0 else dots + dot
    blocks, height, count = out_ref.shape
    cols = height - 16
    lane = lax.broadcasted_iota(jnp.int32, (count, 128), 1)
    high = dots.astype(BF).astype(F32)
    tail = jnp.where(lane == 0, high, jnp.where(lane == 1, dots - high, 0.0)).T[:16].astype(BF)
    terms = terms.T.astype(BF)
    for t in range(blocks):
        out_ref[t, :cols] = terms[t * cols : (t + 1) * cols]
        out_ref[t, cols:] = tail


def pairs(rows, blocks, par, pos, text, image):
    count, width = image.shape
    smem = pl.BlockSpec(memory_space=pltpu.SMEM)
    hbm = pl.BlockSpec(memory_space=pl.ANY)
    return pl.pallas_call(
        lambda *refs: pairs_kernel(rows, *refs),
        in_specs=[smem, smem, hbm, hbm],
        out_specs=pl.BlockSpec(memory_space=pltpu.VMEM),
        out_shape=jax.ShapeDtypeStruct((blocks, width // blocks + 16, count), BF),
        scratch_shapes=[
            pltpu.VMEM(text.shape, BF),
            pltpu.VMEM(image.shape, BF),
            pltpu.SemaphoreType.DMA((3,)),
        ],
        compiler_params=pltpu.CompilerParams(vmem_limit_bytes=56 * 2**20),
        cost_estimate=pl.CostEstimate(
            flops=4 * count * width * text.shape[0],
            bytes_accessed=2 * width * (text.shape[0] + 2 * count),
            transcendentals=count * text.shape[0],
        ),
        name="pairs",
    )(par, pos, text, image)


def per_device(pooled, texts, head_w, log_scale, bias):
    z, yl, c = lax.axis_index("z"), lax.axis_index("yl"), lax.axis_index("c")
    yh, x = lax.axis_index("yh"), lax.axis_index("x")
    rows, width = pooled.shape
    cols = head_w.shape[0]
    scale = jnp.exp(log_scale[0])
    shift = bias[0]

    text_unit = pl.pallas_call(
        unit_kernel, out_shape=jax.ShapeDtypeStruct(texts.shape, BF), name="unit_texts"
    )(texts)
    text_pair = lax.all_gather(text_unit, "yl", axis=0, tiled=True)
    text_all = lax.all_gather(text_pair, ("c", "z"), axis=0, tiled=True)

    images = gather_t(pooled)
    count = images.shape[0]
    own_cols = lax.dot_general(
        head_w, images, (((1,), (1,)), ((), ())), preferred_element_type=F32
    ).astype(BF)
    proj = gather_t(own_cols).reshape(NX, NYH, cols, count)
    proj = proj.transpose(1, 0, 2, 3).reshape(width, count)
    unit_all, norms = unit(proj, 0)
    embedded = unit_all.astype(BF).T

    small = width // (NZ * NYL * NC)
    padded = -(-small // 16) * 16
    parts = images.T.reshape(NZ, NYL * NC, small, count).transpose(1, 0, 2, 3)
    parts = jnp.pad(parts, ((0, 0), (0, 0), (0, padded - small), (0, 0)))
    parts = lax.all_to_all(parts, ("yl", "c"), split_axis=0, concat_axis=0, tiled=True)

    text_all, embedded, norms, parts = lax.optimization_barrier(
        (text_all, embedded, norms, parts)
    )
    par = jnp.stack([scale, shift])
    pos = jnp.stack([((c * NZ + z) * NYL + yl) * rows, (x * NYH + yh) * rows]).astype(jnp.int32)
    block = pairs(rows, NYH * NX, par, pos, text_all, embedded)
    block = lax.all_to_all(block, T, split_axis=0, concat_axis=0, tiled=True)
    block = scale * jnp.sum(block.astype(F32), axis=0)
    row_dots = block[cols : cols + 1] + block[cols + 1 : cols + 2]
    own_unit = own_cols.astype(F32) / norms
    grad_proj = ((block[:cols] - own_unit * row_dots) / norms).astype(BF)

    grad_pooled = lax.dot_general(
        grad_proj, head_w, (((0,), (0,)), ((), ())), preferred_element_type=F32
    ).astype(BF)
    grad_pooled = lax.psum_scatter(grad_pooled, "x", scatter_dimension=0, tiled=True)
    given = jnp.where(yh == 0, grad_pooled[rows:], grad_pooled[:rows])
    kept = jnp.where(yh == 0, grad_pooled[:rows], grad_pooled[rows:])
    given, kept = lax.optimization_barrier((given, kept))
    taken = lax.ppermute(given, "yh", CORES)
    grad_pooled = kept.astype(F32) + taken.astype(F32)

    grad_all = lax.all_gather(grad_proj, ("yl", "c"), axis=0, tiled=True)
    grad_head = pl.pallas_call(
        head_kernel,
        out_shape=jax.ShapeDtypeStruct((NZ, 2 * small, 128), BF),
        compiler_params=pltpu.CompilerParams(vmem_limit_bytes=40 * 2**20),
        cost_estimate=pl.CostEstimate(
            flops=2 * NZ * padded * cols * count * NYL * NC,
            bytes_accessed=2 * (parts.size + grad_all.size + NZ * padded * cols),
            transcendentals=0,
        ),
        name="head_product",
    )(parts, grad_all)
    grad_head = lax.all_to_all(grad_head, "z", split_axis=0, concat_axis=0, tiled=True)
    grad_head, grad_pooled = lax.optimization_barrier((grad_head, grad_pooled))
    grad_head = jnp.sum(grad_head.astype(F32), axis=0)
    grad_head = jnp.concatenate(
        [grad_head[:small], grad_head[small:, : cols - 128]], axis=1
    )
    return (grad_pooled, grad_head)


def solution(mesh):
    fine = Mesh(mesh.devices.reshape(NZ, NYL, NC, NYH, NX), ("z", "yl", "c", "yh", "x"))
    dp = ("z", "yl", "c")
    rows = P(dp + T, None)
    return jax.shard_map(
        per_device,
        mesh=fine,
        in_specs=(rows, rows, P(T, None), P(), P()),
        out_specs=(rows, P(dp, T)),
        check_vma=False,
    )
```

```python
import jax
import jax.numpy as jnp
from jax import lax
from jax.experimental import pallas as pl
from jax.experimental.pallas import tpu as pltpu
from jax.sharding import Mesh, PartitionSpec as P

BF = jnp.bfloat16
F32 = jnp.float32
T = ("yh", "x")
NZ, NYL, NC, NYH, NX = 16, 2, 2, 2, 4
CORES = [(0, 1), (1, 0)]


def unit(v, axis):
    v = v.astype(F32)
    norms = jnp.sqrt(jnp.sum(v * v, axis=axis, keepdims=True) + 1e-06)
    return v / norms, norms


def gather_t(v):
    return lax.all_gather(lax.all_gather(v, "yh", axis=0, tiled=True), "x", axis=0, tiled=True)


def unit_kernel(rows_ref, out_ref):
    v = rows_ref[...].astype(F32)
    out_ref[...] = (v / jnp.sqrt(jnp.sum(v * v, axis=1, keepdims=True) + 1e-06)).astype(BF)


def score(image, text):
    return lax.dot_general(image, text, (((1,), (1,)), ((), ())), preferred_element_type=F32)


def head_kernel(parts_ref, grads_ref, out_ref):
    sources, blocks, height, count = parts_ref.shape
    cols = grads_ref.shape[0] // sources
    total = jnp.zeros((blocks * height, cols), F32)
    for s in range(sources):
        total += score(parts_ref[s].reshape(blocks * height, count), grads_ref[pl.ds(s * cols, cols)])
    total = total.reshape(blocks, height, cols)[:, : out_ref.shape[1] // 2]
    rest = jnp.concatenate(
        [total[:, :, 128:], jnp.zeros((*total.shape[:2], 256 - cols), F32)], axis=2
    )
    out_ref[...] = jnp.concatenate([total[:, :, :128], rest], axis=1).astype(BF)


def pairs_kernel(rows, par_ref, pos_ref, text_hbm, image_hbm, out_ref, text_ref, image_ref, sems):
    blocks, height, count = out_ref.shape
    cols = height - 16
    total, width = text_ref.shape
    parts = [(0, total // 4), (total // 4, total - total // 4)]
    copies = [
        pltpu.make_async_copy(
            text_hbm.at[pl.ds(at, size)], text_ref.at[pl.ds(at, size)], sems.at[k]
        )
        for k, (at, size) in enumerate(parts)
    ]
    image_copy = pltpu.make_async_copy(image_hbm, image_ref, sems.at[len(parts)])
    image_copy.start()
    for copy in copies:
        copy.start()
    image_copy.wait()
    image = image_ref[...]

    def pair_of(k):
        at, size = parts[k]
        copies[k].wait()
        scores = score(image, text_ref[pl.ds(at, size)])
        logits = par_ref[0] * scores + par_ref[1]
        a = lax.broadcasted_iota(jnp.int32, scores.shape, 1) + (at - pos_ref[0])
        b = lax.broadcasted_iota(jnp.int32, scores.shape, 0) - pos_ref[1]
        sign = jnp.where((a == b) & (a >= 0) & (a < rows), -1.0, 1.0)
        pair = (sign / (1.0 + jnp.exp(-sign * logits))).astype(BF)
        return pair, jnp.sum(pair.astype(F32) * scores, axis=1, keepdims=True)

    pair, dots = pair_of(0)
    terms = jnp.dot(pair, text_ref[pl.ds(*parts[0])], preferred_element_type=F32)
    pair, dots_rest = pair_of(1)
    dots += dots_rest
    for at in range(0, width, 256):
        term = jnp.dot(pair, text_ref[pl.ds(*parts[1]), pl.ds(at, 256)], preferred_element_type=F32)
        term = (term + terms[:, at : at + 256]).T.astype(BF)
        row = at
        while row < at + 256:
            t = row // cols
            end = min((t + 1) * cols, at + 256)
            out_ref[t, row - t * cols : end - t * cols] = term[row - at : end - at]
            row = end
    lane = lax.broadcasted_iota(jnp.int32, (count, 128), 1)
    high = dots.astype(BF).astype(F32)
    tail = jnp.where(lane == 0, high, jnp.where(lane == 1, dots - high, 0.0)).T[:16].astype(BF)
    for t in range(blocks):
        out_ref[t, cols:] = tail


def pairs(rows, blocks, par, pos, text, image):
    count, width = image.shape
    smem = pl.BlockSpec(memory_space=pltpu.SMEM)
    hbm = pl.BlockSpec(memory_space=pl.ANY)
    return pl.pallas_call(
        lambda *refs: pairs_kernel(rows, *refs),
        in_specs=[smem, smem, hbm, hbm],
        out_specs=pl.BlockSpec(memory_space=pltpu.VMEM),
        out_shape=jax.ShapeDtypeStruct((blocks, width // blocks + 16, count), BF),
        scratch_shapes=[
            pltpu.VMEM(text.shape, BF),
            pltpu.VMEM(image.shape, BF),
            pltpu.SemaphoreType.DMA((3,)),
        ],
        compiler_params=pltpu.CompilerParams(vmem_limit_bytes=52 * 2**20),
        cost_estimate=pl.CostEstimate(
            flops=4 * count * width * text.shape[0],
            bytes_accessed=2 * width * (text.shape[0] + 2 * count),
            transcendentals=count * text.shape[0],
        ),
        name="pairs",
    )(par, pos, text, image)


def per_device(pooled, texts, head_w, log_scale, bias):
    z, yl, c = lax.axis_index("z"), lax.axis_index("yl"), lax.axis_index("c")
    yh, x = lax.axis_index("yh"), lax.axis_index("x")
    rows, width = pooled.shape
    cols = head_w.shape[0]
    scale = jnp.exp(log_scale[0])
    shift = bias[0]

    text_unit = pl.pallas_call(
        unit_kernel, out_shape=jax.ShapeDtypeStruct(texts.shape, BF), name="unit_texts"
    )(texts)
    text_pair = lax.all_gather(text_unit, "yl", axis=0, tiled=True)
    text_all = lax.all_gather(text_pair, ("c", "z"), axis=0, tiled=True)

    images = gather_t(pooled)
    count = images.shape[0]
    own_cols = lax.dot_general(
        head_w, images, (((1,), (1,)), ((), ())), preferred_element_type=F32
    ).astype(BF)
    proj = gather_t(own_cols).reshape(NX, NYH, cols, count)
    proj = proj.transpose(1, 0, 2, 3).reshape(width, count)
    unit_all, norms = unit(proj, 0)
    embedded = unit_all.astype(BF).T

    small = width // (NZ * NYL * NC)
    padded = -(-small // 16) * 16
    parts = images.T.reshape(NZ, NYL * NC, small, count).transpose(1, 0, 2, 3)
    parts = jnp.pad(parts, ((0, 0), (0, 0), (0, padded - small), (0, 0)))
    parts = lax.all_to_all(parts, ("yl", "c"), split_axis=0, concat_axis=0, tiled=True)

    text_all, embedded, norms, parts = lax.optimization_barrier(
        (text_all, embedded, norms, parts)
    )
    par = jnp.stack([scale, shift])
    pos = jnp.stack([((c * NZ + z) * NYL + yl) * rows, (x * NYH + yh) * rows]).astype(jnp.int32)
    block = pairs(rows, NYH * NX, par, pos, text_all, embedded)
    block = lax.all_to_all(block, T, split_axis=0, concat_axis=0, tiled=True)
    block = scale * jnp.sum(block.astype(F32), axis=0)
    row_dots = block[cols : cols + 1] + block[cols + 1 : cols + 2]
    own_unit = own_cols.astype(F32) / norms
    grad_proj = ((block[:cols] - own_unit * row_dots) / norms).astype(BF)

    grad_pooled = lax.dot_general(
        grad_proj, head_w, (((0,), (0,)), ((), ())), preferred_element_type=F32
    ).astype(BF)
    grad_pooled = lax.psum_scatter(grad_pooled, "x", scatter_dimension=0, tiled=True)
    given = jnp.where(yh == 0, grad_pooled[rows:], grad_pooled[:rows])
    kept = jnp.where(yh == 0, grad_pooled[:rows], grad_pooled[rows:])
    given, kept = lax.optimization_barrier((given, kept))
    taken = lax.ppermute(given, "yh", CORES)
    grad_pooled = kept.astype(F32) + taken.astype(F32)

    grad_all = lax.all_gather(grad_proj, ("yl", "c"), axis=0, tiled=True)
    grad_head = pl.pallas_call(
        head_kernel,
        out_shape=jax.ShapeDtypeStruct((NZ, 2 * small, 128), BF),
        compiler_params=pltpu.CompilerParams(vmem_limit_bytes=40 * 2**20),
        cost_estimate=pl.CostEstimate(
            flops=2 * NZ * padded * cols * count * NYL * NC,
            bytes_accessed=2 * (parts.size + grad_all.size + NZ * padded * cols),
            transcendentals=0,
        ),
        name="head_product",
    )(parts, grad_all)
    grad_head = lax.all_to_all(grad_head, "z", split_axis=0, concat_axis=0, tiled=True)
    grad_head, grad_pooled = lax.optimization_barrier((grad_head, grad_pooled))
    grad_head = jnp.sum(grad_head.astype(F32), axis=0)
    grad_head = jnp.concatenate(
        [grad_head[:small], grad_head[small:, : cols - 128]], axis=1
    )
    return (grad_pooled, grad_head)


def solution(mesh):
    fine = Mesh(mesh.devices.reshape(NZ, NYL, NC, NYH, NX), ("z", "yl", "c", "yh", "x"))
    dp = ("z", "yl", "c")
    rows = P(dp + T, None)
    return jax.shard_map(
        per_device,
        mesh=fine,
        in_specs=(rows, rows, P(T, None), P(), P()),
        out_specs=(rows, P(dp, T)),
        check_vma=False,
    )
```

```python
import jax
import jax.numpy as jnp
from jax import lax
from jax.experimental import pallas as pl
from jax.experimental.pallas import tpu as pltpu
from jax.sharding import Mesh, PartitionSpec as P

BF = jnp.bfloat16
F32 = jnp.float32
T = ("yh", "x")
NZ, NYL, NC, NYH, NX = 16, 2, 2, 2, 4
CORES = [(0, 1), (1, 0)]


def unit(v, axis):
    v = v.astype(F32)
    norms = jnp.sqrt(jnp.sum(v * v, axis=axis, keepdims=True) + 1e-06)
    return v / norms, norms


def gather_t(v):
    return lax.all_gather(lax.all_gather(v, "yh", axis=0, tiled=True), "x", axis=0, tiled=True)


def unit_kernel(rows_ref, out_ref):
    v = rows_ref[...].astype(F32)
    out_ref[...] = (v / jnp.sqrt(jnp.sum(v * v, axis=1, keepdims=True) + 1e-06)).astype(BF)


def score(image, text):
    return lax.dot_general(image, text, (((1,), (1,)), ((), ())), preferred_element_type=F32)


def head_kernel(parts_ref, grads_ref, out_ref):
    sources, blocks, height, count = parts_ref.shape
    cols = grads_ref.shape[0] // sources
    total = jnp.zeros((blocks * height, cols), F32)
    for s in range(sources):
        total += score(parts_ref[s].reshape(blocks * height, count), grads_ref[pl.ds(s * cols, cols)])
    total = total.reshape(blocks, height, cols)[:, : out_ref.shape[1] // 2]
    rest = jnp.concatenate(
        [total[:, :, 128:], jnp.zeros((*total.shape[:2], 256 - cols), F32)], axis=2
    )
    out_ref[...] = jnp.concatenate([total[:, :, :128], rest], axis=1).astype(BF)


def pairs_kernel(rows, par_ref, pos_ref, text_hbm, image_ref, out_ref, text_ref, sems):
    blocks, height = out_ref.shape[0], out_ref.shape[1] // 2
    count, cols = image_ref.shape[0], height - 16
    total, width = text_ref.shape
    parts = [(0, total // 4), (total // 4, total - total // 4)]
    copies = [
        pltpu.make_async_copy(
            text_hbm.at[pl.ds(at, size)], text_ref.at[pl.ds(at, size)], sems.at[k]
        )
        for k, (at, size) in enumerate(parts)
    ]
    for copy in copies:
        copy.start()
    image = image_ref[...]

    def pair_of(k):
        at, size = parts[k]
        copies[k].wait()
        scores = score(image, text_ref[pl.ds(at, size)])
        logits = par_ref[0] * scores + par_ref[1]
        a = lax.broadcasted_iota(jnp.int32, scores.shape, 1) + (at - pos_ref[0])
        b = lax.broadcasted_iota(jnp.int32, scores.shape, 0) - pos_ref[1]
        sign = jnp.where((a == b) & (a >= 0) & (a < rows), -1.0, 1.0)
        pair = (sign / (1.0 + jnp.exp(-sign * logits))).astype(BF)
        return pair, jnp.sum(pair.astype(F32) * scores, axis=1, keepdims=True)

    pair, dots = pair_of(0)
    terms = jnp.dot(pair, text_ref[pl.ds(*parts[0])], preferred_element_type=F32)
    pair, dots_rest = pair_of(1)
    dots += dots_rest
    for at in range(0, width, 256):
        term = jnp.dot(pair, text_ref[pl.ds(*parts[1]), pl.ds(at, 256)], preferred_element_type=F32)
        term = (term + terms[:, at : at + 256]).T.astype(BF)
        row = at
        while row < at + 256:
            t = row // cols
            end = min((t + 1) * cols, at + 256)
            for low in (0, 1):
                out_ref[t, pl.ds(low * height + row - t * cols, end - row)] = term[
                    row - at : end - at, low * 128 : low * 128 + 128
                ]
            row = end
    lane = lax.broadcasted_iota(jnp.int32, (count, 128), 1)
    high = dots.astype(BF).astype(F32)
    tail = jnp.where(lane == 0, high, jnp.where(lane == 1, dots - high, 0.0)).T[:16].astype(BF)
    for t in range(blocks):
        for low in (0, 1):
            out_ref[t, pl.ds(low * height + cols, 16)] = tail[:, low * 128 : low * 128 + 128]


def pairs(rows, blocks, par, pos, text, image):
    count, width = image.shape
    smem = pl.BlockSpec(memory_space=pltpu.SMEM)
    vmem = pl.BlockSpec(memory_space=pltpu.VMEM)
    return pl.pallas_call(
        lambda *refs: pairs_kernel(rows, *refs),
        in_specs=[smem, smem, pl.BlockSpec(memory_space=pl.ANY), vmem],
        out_specs=vmem,
        out_shape=jax.ShapeDtypeStruct((blocks, 2 * (width // blocks + 16), count // 2), BF),
        scratch_shapes=[pltpu.VMEM(text.shape, BF), pltpu.SemaphoreType.DMA((2,))],
        compiler_params=pltpu.CompilerParams(vmem_limit_bytes=52 * 2**20),
        cost_estimate=pl.CostEstimate(
            flops=4 * count * width * text.shape[0],
            bytes_accessed=2 * width * (text.shape[0] + 2 * count),
            transcendentals=count * text.shape[0],
        ),
        name="pairs",
    )(par, pos, text, image)


def per_device(pooled, texts, head_w, log_scale, bias):
    z, yl, c = lax.axis_index("z"), lax.axis_index("yl"), lax.axis_index("c")
    yh, x = lax.axis_index("yh"), lax.axis_index("x")
    rows, width = pooled.shape
    cols = head_w.shape[0]
    scale = jnp.exp(log_scale[0])
    shift = bias[0]

    text_unit = pl.pallas_call(
        unit_kernel, out_shape=jax.ShapeDtypeStruct(texts.shape, BF), name="unit_texts"
    )(texts)
    text_pair = lax.all_gather(text_unit, "yl", axis=0, tiled=True)
    text_all = lax.all_gather(text_pair, ("c", "z"), axis=0, tiled=True)

    images = gather_t(pooled)
    count = images.shape[0]
    own_cols = lax.dot_general(
        head_w, images, (((1,), (1,)), ((), ())), preferred_element_type=F32
    ).astype(BF)
    proj = gather_t(own_cols).reshape(NX, NYH, cols, count)
    proj = proj.transpose(1, 0, 2, 3).reshape(width, count)
    unit_all, norms = unit(proj, 0)
    embedded = unit_all.astype(BF).T

    small = width // (NZ * NYL * NC)
    padded = -(-small // 16) * 16
    parts = images.T.reshape(NZ, NYL * NC, small, count).transpose(1, 0, 2, 3)
    parts = jnp.pad(parts, ((0, 0), (0, 0), (0, padded - small), (0, 0)))
    parts = lax.all_to_all(parts, ("yl", "c"), split_axis=0, concat_axis=0, tiled=True)

    norms = jnp.stack([norms[:, : count // 2], norms[:, count // 2 :]])
    own_unit = jnp.stack([own_cols[:, : count // 2], own_cols[:, count // 2 :]])
    own_unit = own_unit.astype(F32) / norms
    text_all, embedded, norms, own_unit, parts = lax.optimization_barrier(
        (text_all, embedded, norms, own_unit, parts)
    )
    par = jnp.stack([scale, shift])
    pos = jnp.stack([((c * NZ + z) * NYL + yl) * rows, (x * NYH + yh) * rows]).astype(jnp.int32)
    block = pairs(rows, NYH * NX, par, pos, text_all, embedded)
    block = lax.all_to_all(block, T, split_axis=0, concat_axis=0, tiled=True)
    block = scale * jnp.sum(block.astype(F32), axis=0).reshape(2, cols + 16, count // 2)
    row_dots = block[:, cols : cols + 1] + block[:, cols + 1 : cols + 2]
    grad_proj = ((block[:, :cols] - own_unit * row_dots) / norms).astype(BF)
    grad_proj = jnp.concatenate([grad_proj[0], grad_proj[1]], axis=1)

    grad_pooled = lax.dot_general(
        grad_proj, head_w, (((0,), (0,)), ((), ())), preferred_element_type=F32
    ).astype(BF)
    grad_pooled = lax.psum_scatter(grad_pooled, "x", scatter_dimension=0, tiled=True)
    given = jnp.where(yh == 0, grad_pooled[rows:], grad_pooled[:rows])
    kept = jnp.where(yh == 0, grad_pooled[:rows], grad_pooled[rows:])
    given, kept = lax.optimization_barrier((given, kept))
    taken = lax.ppermute(given, "yh", CORES)
    grad_pooled = kept.astype(F32) + taken.astype(F32)

    grad_all = lax.all_gather(grad_proj, ("yl", "c"), axis=0, tiled=True)
    grad_head = pl.pallas_call(
        head_kernel,
        out_shape=jax.ShapeDtypeStruct((NZ, 2 * small, 128), BF),
        compiler_params=pltpu.CompilerParams(vmem_limit_bytes=40 * 2**20),
        cost_estimate=pl.CostEstimate(
            flops=2 * NZ * padded * cols * count * NYL * NC,
            bytes_accessed=2 * (parts.size + grad_all.size + NZ * padded * cols),
            transcendentals=0,
        ),
        name="head_product",
    )(parts, grad_all)
    grad_head = lax.all_to_all(grad_head, "z", split_axis=0, concat_axis=0, tiled=True)
    grad_head, grad_pooled = lax.optimization_barrier((grad_head, grad_pooled))
    grad_head = jnp.sum(grad_head.astype(F32), axis=0)
    grad_head = jnp.concatenate(
        [grad_head[:small], grad_head[small:, : cols - 128]], axis=1
    )
    return (grad_pooled, grad_head)


def solution(mesh):
    fine = Mesh(mesh.devices.reshape(NZ, NYL, NC, NYH, NX), ("z", "yl", "c", "yh", "x"))
    dp = ("z", "yl", "c")
    rows = P(dp + T, None)
    return jax.shard_map(
        per_device,
        mesh=fine,
        in_specs=(rows, rows, P(T, None), P(), P()),
        out_specs=(rows, P(dp, T)),
        check_vma=False,
    )
```

```python
import jax
import jax.numpy as jnp
from jax import lax
from jax.experimental import pallas as pl
from jax.experimental.pallas import tpu as pltpu
from jax.sharding import Mesh, PartitionSpec as P

BF = jnp.bfloat16
F32 = jnp.float32
T = ("yh", "x")
Z = ("zh", "zl")
NZH, NZL, NYL, NC, NYH, NX = 2, 8, 2, 2, 2, 4
NZ = NZH * NZL
CORES = [(0, 1), (1, 0)]


def unit(v, axis):
    v = v.astype(F32)
    norms = jnp.sqrt(jnp.sum(v * v, axis=axis, keepdims=True) + 1e-06)
    return v / norms, norms


def gather_t(v):
    return lax.all_gather(lax.all_gather(v, "yh", axis=0, tiled=True), "x", axis=0, tiled=True)


def unit_kernel(rows_ref, out_ref):
    v = rows_ref[...].astype(F32)
    out_ref[...] = (v / jnp.sqrt(jnp.sum(v * v, axis=1, keepdims=True) + 1e-06)).astype(BF)


def score(image, text):
    return lax.dot_general(image, text, (((1,), (1,)), ((), ())), preferred_element_type=F32)


def head_kernel(parts_ref, grads_ref, out_ref):
    sources, blocks, height, count = parts_ref.shape
    cols = grads_ref.shape[0] // sources
    total = jnp.zeros((blocks * height, cols), F32)
    for s in range(sources):
        total += score(parts_ref[s].reshape(blocks * height, count), grads_ref[pl.ds(s * cols, cols)])
    total = total.reshape(blocks, height, cols)[:, : out_ref.shape[1] // 2]
    rest = jnp.concatenate(
        [total[:, :, 128:], jnp.zeros((*total.shape[:2], 256 - cols), F32)], axis=2
    )
    out_ref[...] = jnp.concatenate([total[:, :, :128], rest], axis=1).astype(BF)


def slot(t):
    return t % NX * NYH + t // NX


def pairs_kernel(rows, par_ref, pos_ref, text_hbm, image_ref, out_ref, text_ref, sems):
    blocks, height = out_ref.shape[0], out_ref.shape[1] // 2
    count, cols = image_ref.shape[0], height - 16
    total, width = text_ref.shape
    parts = [(0, total // 4), (total // 4, total - total // 4)]
    copies = [
        pltpu.make_async_copy(
            text_hbm.at[pl.ds(at, size)], text_ref.at[pl.ds(at, size)], sems.at[k]
        )
        for k, (at, size) in enumerate(parts)
    ]
    for copy in copies:
        copy.start()
    image = image_ref[...]

    def pair_of(k):
        at, size = parts[k]
        copies[k].wait()
        scores = score(image, text_ref[pl.ds(at, size)])
        logits = par_ref[0] * scores + par_ref[1]
        a = lax.broadcasted_iota(jnp.int32, scores.shape, 1) + (at - pos_ref[0])
        b = lax.broadcasted_iota(jnp.int32, scores.shape, 0) - pos_ref[1]
        sign = jnp.where((a == b) & (a >= 0) & (a < rows), -1.0, 1.0)
        pair = (sign / (1.0 + jnp.exp(-sign * logits))).astype(BF)
        return pair, jnp.sum(pair.astype(F32) * scores, axis=1, keepdims=True)

    pair, dots = pair_of(0)
    terms = jnp.dot(pair, text_ref[pl.ds(*parts[0])], preferred_element_type=F32)
    pair, dots_rest = pair_of(1)
    dots += dots_rest
    for at in range(0, width, 256):
        term = jnp.dot(pair, text_ref[pl.ds(*parts[1]), pl.ds(at, 256)], preferred_element_type=F32)
        term = (term + terms[:, at : at + 256]).T.astype(BF)
        row = at
        while row < at + 256:
            t = row // cols
            end = min((t + 1) * cols, at + 256)
            for low in (0, 1):
                out_ref[slot(t), pl.ds(low * height + row - t * cols, end - row)] = term[
                    row - at : end - at, low * 128 : low * 128 + 128
                ]
            row = end
    lane = lax.broadcasted_iota(jnp.int32, (count, 128), 1)
    high = dots.astype(BF).astype(F32)
    tail = jnp.where(lane == 0, high, jnp.where(lane == 1, dots - high, 0.0)).T[:16].astype(BF)
    for t in range(blocks):
        for low in (0, 1):
            out_ref[t, pl.ds(low * height + cols, 16)] = tail[:, low * 128 : low * 128 + 128]


def pairs(rows, blocks, par, pos, text, image):
    count, width = image.shape
    smem = pl.BlockSpec(memory_space=pltpu.SMEM)
    vmem = pl.BlockSpec(memory_space=pltpu.VMEM)
    return pl.pallas_call(
        lambda *refs: pairs_kernel(rows, *refs),
        in_specs=[smem, smem, pl.BlockSpec(memory_space=pl.ANY), vmem],
        out_specs=vmem,
        out_shape=jax.ShapeDtypeStruct((blocks, 2 * (width // blocks + 16), count // 2), BF),
        scratch_shapes=[pltpu.VMEM(text.shape, BF), pltpu.SemaphoreType.DMA((2,))],
        compiler_params=pltpu.CompilerParams(vmem_limit_bytes=52 * 2**20),
        cost_estimate=pl.CostEstimate(
            flops=4 * count * width * text.shape[0],
            bytes_accessed=2 * width * (text.shape[0] + 2 * count),
            transcendentals=count * text.shape[0],
        ),
        name="pairs",
    )(par, pos, text, image)


def per_device(pooled, texts, head_w, log_scale, bias):
    z, yl, c = lax.axis_index(Z), lax.axis_index("yl"), lax.axis_index("c")
    yh, x = lax.axis_index("yh"), lax.axis_index("x")
    rows, width = pooled.shape
    cols = head_w.shape[0]
    scale = jnp.exp(log_scale[0])
    shift = bias[0]

    text_unit = pl.pallas_call(
        unit_kernel, out_shape=jax.ShapeDtypeStruct(texts.shape, BF), name="unit_texts"
    )(texts)
    text_pair = lax.all_gather(text_unit, "yl", axis=0, tiled=True)
    text_all = lax.all_gather(text_pair, ("c", *Z), axis=0, tiled=True)

    images = gather_t(pooled)
    count = images.shape[0]
    own_cols = lax.dot_general(
        head_w, images, (((1,), (1,)), ((), ())), preferred_element_type=F32
    ).astype(BF)
    proj = gather_t(own_cols).reshape(NX, NYH, cols, count)
    proj = proj.transpose(1, 0, 2, 3).reshape(width, count)
    unit_all, norms = unit(proj, 0)
    embedded = unit_all.astype(BF).T

    small = width // (NZ * NYL * NC)
    padded = -(-small // 16) * 16
    parts = images.T.reshape(NZH, NZL, NYL * NC, small, count).transpose(2, 1, 0, 3, 4)
    parts = parts.reshape(NYL * NC, NZ, small, count)
    parts = jnp.pad(parts, ((0, 0), (0, 0), (0, padded - small), (0, 0)))
    parts = lax.all_to_all(parts, ("yl", "c"), split_axis=0, concat_axis=0, tiled=True)

    norms = jnp.stack([norms[:, : count // 2], norms[:, count // 2 :]])
    own_unit = jnp.stack([own_cols[:, : count // 2], own_cols[:, count // 2 :]])
    own_unit = own_unit.astype(F32) / norms
    text_all, embedded, norms, own_unit, parts = lax.optimization_barrier(
        (text_all, embedded, norms, own_unit, parts)
    )
    par = jnp.stack([scale, shift])
    pos = jnp.stack([((c * NZ + z) * NYL + yl) * rows, (x * NYH + yh) * rows]).astype(jnp.int32)
    block = pairs(rows, NYH * NX, par, pos, text_all, embedded)
    block = lax.all_to_all(block, ("x", "yh"), split_axis=0, concat_axis=0, tiled=True)
    block = scale * jnp.sum(block.astype(F32), axis=0).reshape(2, cols + 16, count // 2)
    row_dots = block[:, cols : cols + 1] + block[:, cols + 1 : cols + 2]
    grad_proj = ((block[:, :cols] - own_unit * row_dots) / norms).astype(BF)
    grad_proj = jnp.concatenate([grad_proj[0], grad_proj[1]], axis=1)

    grad_pooled = lax.dot_general(
        grad_proj, head_w, (((0,), (0,)), ((), ())), preferred_element_type=F32
    ).astype(BF)
    grad_pooled = lax.psum_scatter(grad_pooled, "x", scatter_dimension=0, tiled=True)
    given = jnp.where(yh == 0, grad_pooled[rows:], grad_pooled[:rows])
    kept = jnp.where(yh == 0, grad_pooled[:rows], grad_pooled[rows:])
    given, kept = lax.optimization_barrier((given, kept))
    taken = lax.ppermute(given, "yh", CORES)
    grad_pooled = kept.astype(F32) + taken.astype(F32)

    grad_all = lax.all_gather(grad_proj, ("yl", "c"), axis=0, tiled=True)
    grad_head = pl.pallas_call(
        head_kernel,
        out_shape=jax.ShapeDtypeStruct((NZ, 2 * small, 128), BF),
        compiler_params=pltpu.CompilerParams(vmem_limit_bytes=40 * 2**20),
        cost_estimate=pl.CostEstimate(
            flops=2 * NZ * padded * cols * count * NYL * NC,
            bytes_accessed=2 * (parts.size + grad_all.size + NZ * padded * cols),
            transcendentals=0,
        ),
        name="head_product",
    )(parts, grad_all)
    grad_head = lax.all_to_all(grad_head, ("zl", "zh"), split_axis=0, concat_axis=0, tiled=True)
    grad_head = jnp.sum(grad_head.astype(F32), axis=0)
    grad_head = jnp.concatenate(
        [grad_head[:small], grad_head[small:, : cols - 128]], axis=1
    )
    return (grad_pooled, grad_head)


def solution(mesh):
    fine = Mesh(
        mesh.devices.reshape(NZH, NZL, NYL, NC, NYH, NX), ("zh", "zl", "yl", "c", "yh", "x")
    )
    dp = (*Z, "yl", "c")
    rows = P(dp + T, None)
    return jax.shard_map(
        per_device,
        mesh=fine,
        in_specs=(rows, rows, P(T, None), P(), P()),
        out_specs=(rows, P(dp, T)),
        check_vma=False,
    )
```
